32 devices in a mesh: fsdp: 4 (over z), own: 8 (over y, x, core).
Axes of the slice: x: 2, y: 2, z: 4, core: 2. Of those that a mesh axis runs over, the one named last changes fastest.
Arguments:
- activations: bfloat16 [8192, 8192], P('own', 'fsdp'), may hold values from -6 to 6
- cotangent: bfloat16 [8192, 2048], P('own', 'fsdp'), may hold values from -6 to 6
- frozen_weight: bfloat16 [8192, 2048], P('fsdp', 'own'), may hold values from -0.0625 to 0.0625
- down_weight: bfloat16 [32, 8192, 128], P('own', 'fsdp'), may hold values from -0.0625 to 0.0625
- up_weight: bfloat16 [32, 64, 2048], P('own', None, 'fsdp'), may hold values from -0.1875 to 0.1875
- slot_of_adapter: int32 [32], replicated, may hold values from 0 to 31, as said below
- tenant_of_block: int32 [64], replicated, may hold values from 0 to 31, as said below
Outputs:
- activation_gradient: bfloat16 [8192, 8192], P('own', 'fsdp')
- down_gradient: bfloat16 [32, 8192, 128], P('own', 'fsdp')
- up_gradient: bfloat16 [32, 64, 2048], P('own', None, 'fsdp')
The draws below stay inside these ranges and needn't reach their ends.
Inputs may be any that keep to these rules, and one draw needn't show every extreme that they name: A permutation of the slots: the adapter t is held in row slot_of_adapter[t] of down_weight and up_weight, which lies on own index slot_of_adapter[t] // 4. `tenant_of_block`: bin b holds blocks b * 8 to (b + 1) * 8 - 1. Within a bin the blocks of one adapter stand in one run, and two blocks whose adapters lie on the same own index have the same adapter.
All inputs are finite; a program needn't handle non-finite values.
Results may differ from the reference program's by a relative error of at most 0.0057.
Values may be sent and summed in bfloat16 or wider, within the bound.
A program may use at most 128 MiB of HBM per device.

```python
import jax
import jax.numpy as jnp
from jax import lax

MODEL_WIDTH = 8192
KEY_VALUE_WIDTH = 1024
ADAPTER_RANK = 64
BLOCK = 128
BLK_BIN = 8
ADP_OWN = 4
TOKENS = 8192
ADAPTER_COUNT = 32


def plan_tables(key):
    base_key = jax.random.fold_in(key, 4242)
    slot_key, owner_key, start_key, local_key = jax.random.split(base_key, 4)
    bin_count = ADAPTER_COUNT // ADP_OWN
    slot_table = jax.random.permutation(slot_key, ADAPTER_COUNT).astype(jnp.int32)
    inverse = jnp.argsort(slot_table, stable=True).astype(jnp.int32)

    def owner_row(row_key):
        return jax.random.permutation(row_key, bin_count).astype(jnp.int32)
    owner_perm = jax.vmap(owner_row)(jax.random.split(owner_key, bin_count))
    starts = jax.random.randint(start_key, (bin_count, BLK_BIN), 0, 16) > 0
    starts = starts.at[:, 0].set(True)
    segment = jnp.minimum(jnp.cumsum(starts.astype(jnp.int32), axis=1) - 1, bin_count - 1)
    owner_block = jnp.take_along_axis(owner_perm, segment, axis=1)
    local_seg = jax.random.randint(local_key, (bin_count, bin_count), 0, ADP_OWN).astype(jnp.int32)
    local_block = jnp.take_along_axis(local_seg, segment, axis=1)
    tenant = inverse[(owner_block * ADP_OWN + local_block).reshape(-1)]
    return (slot_table, tenant.astype(jnp.int32))


def draw_slot_of_adapter(key, part):
    return plan_tables(key)[0]


def draw_tenant_of_block(key, part):
    return plan_tables(key)[1]


def steps_of(key, shape, shards, low, high):
    def one(dim, parts):
        heights = jax.random.uniform(jax.random.fold_in(jax.random.fold_in(key, 6), dim), (parts,), jnp.float32, low / len(shards), high / len(shards))
        return jnp.repeat(jnp.exp(heights), shape[dim] // parts).reshape((-1,) + (1,) * (len(shape) - dim - 1))

    factor_of = one(*shards[0])
    for cut in shards[1:]:
        factor_of = factor_of * one(*cut)
    return factor_of


def normal_values(key, extent, width, most, cuts=(), held_as=jnp.bfloat16):
    level = steps_of(key, extent, cuts, -0.22, 0.18) if cuts else 1.0
    drawn = jax.random.normal(key, extent, jnp.float32) * width * level
    return jnp.minimum(jnp.maximum(drawn, -most), most).astype(held_as)


def setup_inputs(seed: int = 0) -> dict:
    key_of = jax.random.split(jax.random.key(seed), 8)
    activations = normal_values(key_of[0], (TOKENS, MODEL_WIDTH), 1.0, 6.0, ((0, 8), (1, 4)))
    cotangent = normal_values(key_of[1], (TOKENS, 2 * KEY_VALUE_WIDTH), 1.0, 6.0, ((0, 8), (1, 4)))
    frozen_weight = normal_values(key_of[2], (MODEL_WIDTH, 2 * KEY_VALUE_WIDTH), MODEL_WIDTH ** -0.5, 0.0625, ((0, 4), (1, 8)))
    down_weight = normal_values(key_of[3], (ADAPTER_COUNT, MODEL_WIDTH, 2 * ADAPTER_RANK), MODEL_WIDTH ** -0.5, 0.0625, ((0, 8), (1, 4)))
    up_weight = normal_values(key_of[4], (ADAPTER_COUNT, ADAPTER_RANK, 2 * KEY_VALUE_WIDTH), KEY_VALUE_WIDTH ** -0.5, 0.1875, ((0, 8), (2, 4)))
    slot_of_adapter = draw_slot_of_adapter(jax.random.fold_in(key_of[7], 71), 0)
    tenant_of_block = draw_tenant_of_block(jax.random.fold_in(key_of[7], 71), 0)
    return dict(activations=activations, cotangent=cotangent, frozen_weight=frozen_weight, down_weight=down_weight, up_weight=up_weight, slot_of_adapter=slot_of_adapter, tenant_of_block=tenant_of_block)


def reference(activations, cotangent, frozen_weight, down_weight, up_weight, slot_of_adapter, tenant_of_block):
    token_bin_index = BLK_BIN * BLOCK
    bin_count = activations.shape[0] // token_bin_index
    slot_rows = slot_of_adapter[tenant_of_block].reshape(bin_count, BLK_BIN).astype(jnp.int32)
    x_bins = activations.reshape(bin_count, token_bin_index, MODEL_WIDTH)
    g_bins = cotangent.reshape(bin_count, token_bin_index, 2 * KEY_VALUE_WIDTH)

    def per_bin(carry, inputs):
        acc_a, acc_b = carry
        x_bin, g_bin, slot_indices = inputs
        adapter_down = down_weight[slot_indices].astype(jnp.float32)
        adapter_up = up_weight[slot_indices].astype(jnp.float32)
        x_blocks = x_bin.reshape(BLK_BIN, BLOCK, MODEL_WIDTH).astype(jnp.float32)
        g_blocks = g_bin.reshape(BLK_BIN, BLOCK, 2 * KEY_VALUE_WIDTH).astype(jnp.float32)
        inner = jnp.einsum('btd,bdr->btr', x_blocks, adapter_down).astype(jnp.bfloat16)
        q_key = jnp.einsum('btc,brc->btr', g_blocks[:, :, :KEY_VALUE_WIDTH], adapter_up[:, :, :KEY_VALUE_WIDTH])
        q_value = jnp.einsum('btc,brc->btr', g_blocks[:, :, KEY_VALUE_WIDTH:], adapter_up[:, :, KEY_VALUE_WIDTH:])
        reduced_rows = jnp.concatenate([q_key, q_value], axis=2).astype(jnp.bfloat16)
        frozen_output = jnp.dot(g_bin, frozen_weight.T, preferred_element_type=jnp.float32)
        adapter_output = jnp.einsum('mch,myh->mcy', reduced_rows.astype(jnp.float32), adapter_down).reshape(token_bin_index, MODEL_WIDTH)
        activation_gradient = (frozen_output + adapter_output).astype(jnp.bfloat16)
        part_a = jnp.einsum('btd,btr->bdr', x_blocks, reduced_rows.astype(jnp.float32))
        inner_f = inner.astype(jnp.float32)
        part_b = jnp.concatenate([
            jnp.einsum('btr,btc->brc', inner_f[:, :, :ADAPTER_RANK], g_blocks[:, :, :KEY_VALUE_WIDTH]),
            jnp.einsum('btr,btc->brc', inner_f[:, :, ADAPTER_RANK:], g_blocks[:, :, KEY_VALUE_WIDTH:])], axis=2)
        same = (slot_indices[:, None] == slot_indices[None, :]).astype(jnp.float32)
        leading = jnp.concatenate([jnp.ones((1,), jnp.bool_), slot_indices[1:] != slot_indices[:-1]]).astype(jnp.float32)
        merged_a = jnp.einsum('jk,kdr->jdr', same, part_a, precision=lax.Precision.HIGHEST)
        merged_b = jnp.einsum('jk,kdr->jdr', same, part_b, precision=lax.Precision.HIGHEST)
        merged_a = lax.optimization_barrier(merged_a.astype(jnp.bfloat16)).astype(jnp.float32)
        merged_b = lax.optimization_barrier(merged_b.astype(jnp.bfloat16)).astype(jnp.float32)
        acc_a = acc_a.at[slot_indices].add(merged_a * leading[:, None, None])
        acc_b = acc_b.at[slot_indices].add(merged_b * leading[:, None, None])
        return (acc_a, acc_b), activation_gradient

    start = (jnp.zeros((ADAPTER_COUNT, MODEL_WIDTH, 2 * ADAPTER_RANK), jnp.float32), jnp.zeros((ADAPTER_COUNT, ADAPTER_RANK, 2 * KEY_VALUE_WIDTH), jnp.float32))
    (acc_a, acc_b), grads = lax.scan(per_bin, start, (x_bins, g_bins, slot_rows))
    return grads.reshape(bin_count * token_bin_index, MODEL_WIDTH), acc_a.astype(jnp.bfloat16), acc_b.astype(jnp.bfloat16)
```

```python
import jax
import jax.numpy as jnp
from jax import lax
from jax.experimental import pallas as pl
from jax.experimental.pallas import tpu as pltpu
from jax.sharding import PartitionSpec as P

KEY_VALUE_WIDTH = 1024
BLOCK = 128


def copy_body(index_ref, from_ref, to_ref):
    to_ref[...] = from_ref[...]


def pick_rows(index, stacked):
    shape = (1,) + stacked.shape[1:]
    return pl.pallas_call(
        copy_body,
        grid_spec=pltpu.PrefetchScalarGridSpec(
            num_scalar_prefetch=1,
            grid=(index.shape[0],),
            in_specs=[pl.BlockSpec(shape, lambda k, index_ref: (index_ref[k], 0, 0))],
            out_specs=pl.BlockSpec(shape, lambda k, index_ref: (k, 0, 0)),
        ),
        out_shape=jax.ShapeDtypeStruct(index.shape + stacked.shape[1:], stacked.dtype),
    )(index, stacked)


def inner_body(index_ref, x_ref, a_ref, out_ref):
    out_ref[...] = jnp.dot(x_ref[...], a_ref[0], preferred_element_type=jnp.float32).astype(
        out_ref.dtype
    )


def inner_product(index, tokens, maps):
    rows, width = tokens.shape
    rank = maps.shape[2]
    return pl.pallas_call(
        inner_body,
        grid_spec=pltpu.PrefetchScalarGridSpec(
            num_scalar_prefetch=1,
            grid=(index.shape[0],),
            in_specs=[
                pl.BlockSpec((BLOCK, width), lambda k, index_ref: (k, 0)),
                pl.BlockSpec((1, width, rank), lambda k, index_ref: (index_ref[k], 0, 0)),
            ],
            out_specs=pl.BlockSpec((BLOCK, rank), lambda k, index_ref: (k, 0)),
        ),
        out_shape=jax.ShapeDtypeStruct((rows, rank), jnp.bfloat16),
    )(index, tokens, maps)


def after(value, *others):
    return lax.optimization_barrier((value,) + others)[0]


def shards(
    activations, cotangent, frozen_weight, down_weight, up_weight, slot_of_adapter, tenant_of_block
):
    own_count = lax.axis_size("own")
    own_index = lax.axis_index("own")
    fsdp_count = lax.axis_size("fsdp")
    fsdp_index = lax.axis_index("fsdp")
    tok_rows, width_part = activations.shape
    col_count = cotangent.shape[1]
    resident_count = down_weight.shape[0]
    paired_rank = down_weight.shape[2]
    rank_half = paired_rank // 2
    block_count = tok_rows // BLOCK
    slot_table = slot_of_adapter[tenant_of_block].reshape(own_count, block_count)
    owner_table = slot_table // resident_count
    local_table = slot_table % resident_count
    wanted_mask = owner_table == own_index
    wanted_any = jnp.any(wanted_mask, axis=1)
    wanted_local = jnp.max(jnp.where(wanted_mask, local_table, 0), axis=1)
    held_ids = jnp.arange(resident_count, dtype=jnp.int32)
    serve_mask = (wanted_local[:, None] == held_ids[None, :]) & wanted_any[:, None]
    my_owner = lax.dynamic_index_in_dim(owner_table, own_index, 0, keepdims=False)
    owner_ids = jnp.arange(own_count, dtype=jnp.int32)
    owner_rows = jnp.repeat(my_owner, BLOCK)
    row_mask = owner_ids[:, None] == owner_rows[None, :]

    def exchange(value):
        return lax.all_to_all(value, "own", split_axis=0, concat_axis=0, tiled=True)

    fetched_b = exchange(pick_rows(wanted_local, up_weight))
    outgoing_down = after(pick_rows(wanted_local, down_weight), fetched_b)
    fetched_a = exchange(outgoing_down)

    g_blocks = cotangent.reshape(block_count, BLOCK, col_count)
    block_b = fetched_b[my_owner]
    q_single = jnp.einsum(
        "btc,brc->btr", g_blocks, block_b, preferred_element_type=jnp.float32
    ).reshape(tok_rows, rank_half)
    q_all = lax.all_gather(q_single.astype(jnp.bfloat16), "fsdp", axis=0)
    q_low = (
        q_all.reshape(2, fsdp_count // 2, tok_rows, rank_half)
        .astype(jnp.float32)
        .sum(axis=1)
        .astype(jnp.bfloat16)
    )
    q_low = jnp.concatenate([q_low[0], q_low[1]], axis=1)
    q_wide = jnp.where(row_mask[:, :, None], q_low[None], jnp.bfloat16(0))

    weight_rows = lax.all_gather(frozen_weight, "own", axis=1, tiled=True)
    full_grad = lax.all_gather(cotangent, "fsdp", axis=1, tiled=True)

    part_a = jnp.einsum(
        "otr,td->ord", q_wide, activations, preferred_element_type=jnp.float32
    ).astype(jnp.bfloat16)
    fetched_a, part_a, weight_rows = lax.optimization_barrier((fetched_a, part_a, weight_rows))
    back_a = exchange(part_a)

    inner_part = inner_product(my_owner, activations, fetched_a)
    inner_all = lax.all_gather(inner_part, "fsdp", axis=0)
    proj_index = fsdp_index * col_count // KEY_VALUE_WIDTH
    inner_mine = lax.dynamic_slice_in_dim(inner_all, proj_index * rank_half, rank_half, 2)
    inner_mine = inner_mine.astype(jnp.float32).sum(axis=0).astype(jnp.bfloat16)
    inner_wide = jnp.where(row_mask[:, :, None], inner_mine[None], jnp.bfloat16(0))
    part_b = jnp.einsum(
        "otr,tc->orc", inner_wide, cotangent, preferred_element_type=jnp.float32
    ).astype(jnp.bfloat16)

    block_a = fetched_a[my_owner]
    q_blocks = q_low.reshape(block_count, BLOCK, paired_rank)
    frozen_gradient = lax.dot_general(
        full_grad, weight_rows, (((1,), (1,)), ((), ())), preferred_element_type=jnp.float32
    )
    adapter_gradient = jnp.einsum(
        "mch,myh->mcy", q_blocks, block_a, preferred_element_type=jnp.float32
    ).reshape(tok_rows, width_part)
    activation_gradient = (frozen_gradient + adapter_gradient).astype(jnp.bfloat16)

    def accumulate(back):
        terms = jnp.where(serve_mask[:, :, None, None], back[:, None], jnp.bfloat16(0))
        return terms.astype(jnp.float32).sum(axis=0).astype(jnp.bfloat16)

    down_gradient = accumulate(after(back_a, activation_gradient)).transpose(0, 2, 1)
    back_b = exchange(after(part_b, back_a))
    up_gradient = accumulate(back_b)
    return (activation_gradient, down_gradient, up_gradient)


def solution(mesh):
    return jax.shard_map(
        shards,
        mesh=mesh,
        in_specs=(
            P("own", "fsdp"),
            P("own", "fsdp"),
            P("fsdp", "own"),
            P("own", "fsdp", None),
            P("own", None, "fsdp"),
            P(),
            P(),
        ),
        out_specs=(P("own", "fsdp"), P("own", "fsdp", None), P("own", None, "fsdp")),
        check_vma=False,
    )
```

```python
import functools

import jax
import jax.numpy as jnp
from jax import lax
from jax.experimental import pallas as pl
from jax.experimental.pallas import tpu as pltpu
from jax.sharding import PartitionSpec as P

KEY_VALUE_WIDTH = 1024
BLOCK = 128
MESH = pl.DeviceIdType.MESH


def copy_body(index_ref, from_ref, to_ref):
    to_ref[...] = from_ref[...]


def pick_rows(index, stacked):
    shape = (1,) + stacked.shape[1:]
    return pl.pallas_call(
        copy_body,
        grid_spec=pltpu.PrefetchScalarGridSpec(
            num_scalar_prefetch=1,
            grid=(index.shape[0],),
            in_specs=[pl.BlockSpec(shape, lambda k, index_ref: (index_ref[k], 0, 0))],
            out_specs=pl.BlockSpec(shape, lambda k, index_ref: (k, 0, 0)),
        ),
        out_shape=jax.ShapeDtypeStruct(index.shape + stacked.shape[1:], stacked.dtype),
    )(index, stacked)


def inner_body(index_ref, x_ref, a_ref, out_ref):
    out_ref[...] = jnp.dot(x_ref[...], a_ref[0], preferred_element_type=jnp.float32).astype(
        out_ref.dtype
    )


def inner_product(index, tokens, maps):
    rows, width = tokens.shape
    rank = maps.shape[2]
    return pl.pallas_call(
        inner_body,
        grid_spec=pltpu.PrefetchScalarGridSpec(
            num_scalar_prefetch=1,
            grid=(index.shape[0],),
            in_specs=[
                pl.BlockSpec((BLOCK, width), lambda k, index_ref: (k, 0)),
                pl.BlockSpec((1, width, rank), lambda k, index_ref: (index_ref[k], 0, 0)),
            ],
            out_specs=pl.BlockSpec((BLOCK, rank), lambda k, index_ref: (k, 0)),
        ),
        out_shape=jax.ShapeDtypeStruct((rows, rank), jnp.bfloat16),
    )(index, tokens, maps)


def gather_body(chips, ring, w_ref, g_ref, w_out, g_out, w_send, w_recv, f_send, f_recv, g_send, g_recv, here):
    own = lax.axis_index("own")
    fsdp = lax.axis_index("fsdp")
    chip, core = own // 2, lax.rem(own, 2)
    sibling = chip * 2 + 1 - core
    columns = g_ref.shape[1]

    def chip_of(k):
        return lax.rem(chip + k, chips)

    def g_slice(f):
        return g_out.at[:, pl.ds(pl.multiple_of(f * columns, columns), columns)]

    keep_w = pltpu.make_async_copy(w_ref, w_out.at[own], here.at[0])
    keep_g = pltpu.make_async_copy(g_ref, g_slice(fsdp), here.at[1])
    keep_w.start()
    keep_g.start()

    barrier = pltpu.get_barrier_semaphore()
    for k in range(1, chips):
        pl.semaphore_signal(
            barrier, inc=1, device_id={"own": chip_of(k) * 2 + core}, device_id_type=MESH
        )
    pl.semaphore_signal(barrier, inc=1, device_id={"own": sibling}, device_id_type=MESH)

    @pl.when(fsdp > 0)
    def _():
        pl.semaphore_signal(barrier, inc=1, device_id={"fsdp": fsdp - 1}, device_id_type=MESH)

    @pl.when(fsdp < ring - 1)
    def _():
        pl.semaphore_signal(barrier, inc=1, device_id={"fsdp": fsdp + 1}, device_id_type=MESH)

    inside = (fsdp > 0).astype(jnp.int32) + (fsdp < ring - 1).astype(jnp.int32)
    pl.semaphore_wait(barrier, chips + inside)

    def g_copy(way, k):
        sign = 1 if way == 0 else -1
        origin = fsdp - sign * k
        return pltpu.make_async_remote_copy(
            src_ref=g_ref if k == 0 else g_slice(origin),
            dst_ref=g_slice(origin),
            send_sem=g_send.at[way, k],
            recv_sem=g_recv.at[way, k],
            device_id={"fsdp": fsdp + sign},
            device_id_type=MESH,
        )

    def g_arrival(way, k):
        sign = 1 if way == 0 else -1
        origin = fsdp - sign * (k + 1)
        return pltpu.make_async_remote_copy(
            src_ref=g_slice(origin),
            dst_ref=g_slice(origin),
            send_sem=g_send.at[way, k],
            recv_sem=g_recv.at[way, k],
            device_id={"fsdp": fsdp - sign},
            device_id_type=MESH,
        )

    def g_sends(way, k):
        if way == 0:
            return (fsdp >= k) & (fsdp < ring - 1)
        return (fsdp <= ring - 1 - k) & (fsdp > 0)

    def g_gets(way, k):
        return fsdp >= k + 1 if way == 0 else fsdp <= ring - 2 - k

    def w_copy(k):
        return pltpu.make_async_remote_copy(
            src_ref=w_ref,
            dst_ref=w_out.at[own],
            send_sem=w_send.at[k - 1],
            recv_sem=w_recv.at[k - 1],
            device_id={"own": chip_of(k) * 2 + core},
            device_id_type=MESH,
        )

    def w_origin(k, side):
        return lax.rem(chip + chips - k, chips) * 2 + side

    def w_forward(k):
        piece = w_origin(k, core)
        return pltpu.make_async_remote_copy(
            src_ref=w_ref if k == 0 else w_out.at[piece],
            dst_ref=w_out.at[piece],
            send_sem=f_send.at[k],
            recv_sem=f_recv.at[k],
            device_id={"own": sibling},
            device_id_type=MESH,
        )

    for way in range(2):
        @pl.when(g_sends(way, 0))
        def _():
            g_copy(way, 0).start()

    for k in range(1, chips):
        w_copy(k).start()
    w_forward(0).start()

    for k in range(max(ring - 1, chips - 1)):
        if k < ring - 1:
            for way in range(2):
                @pl.when(g_gets(way, k))
                def _():
                    g_arrival(way, k).wait_recv()

                if k + 1 < ring - 1:
                    @pl.when(g_sends(way, k + 1))
                    def _():
                        g_copy(way, k + 1).start()
        if k < chips - 1:
            piece = w_origin(k + 1, core)
            pltpu.make_async_remote_copy(
                src_ref=w_ref,
                dst_ref=w_out.at[piece],
                send_sem=w_send.at[k],
                recv_sem=w_recv.at[k],
                device_id={"own": sibling},
                device_id_type=MESH,
            ).wait_recv()
            w_forward(k + 1).start()

    for k in range(chips):
        piece = w_origin(k, 1 - core)
        pltpu.make_async_remote_copy(
            src_ref=w_ref,
            dst_ref=w_out.at[piece],
            send_sem=f_send.at[k],
            recv_sem=f_recv.at[k],
            device_id={"own": sibling},
            device_id_type=MESH,
        ).wait_recv()
        w_forward(k).wait_send()
    for k in range(1, chips):
        w_copy(k).wait_send()
    for k in range(ring - 1):
        for way in range(2):
            @pl.when(g_sends(way, k))
            def _():
                g_copy(way, k).wait_send()
    keep_w.wait()
    keep_g.wait()


def gather(weight, cotangent):
    own_count, ring = lax.axis_size("own"), lax.axis_size("fsdp")
    chips = own_count // 2
    hbm = pl.BlockSpec(memory_space=pl.ANY)
    dma = pltpu.SemaphoreType.DMA
    return pl.pallas_call(
        functools.partial(gather_body, chips, ring),
        out_shape=(
            jax.ShapeDtypeStruct((own_count,) + weight.shape, weight.dtype),
            jax.ShapeDtypeStruct((cotangent.shape[0], cotangent.shape[1] * ring), cotangent.dtype),
        ),
        in_specs=[hbm, hbm],
        out_specs=(hbm, hbm),
        scratch_shapes=[
            dma((chips - 1,)),
            dma((chips - 1,)),
            dma((chips,)),
            dma((chips,)),
            dma((2, ring - 1)),
            dma((2, ring - 1)),
            dma((2,)),
        ],
        compiler_params=pltpu.CompilerParams(collective_id=0, has_side_effects=True),
    )(weight, cotangent)


def grad_body(index_ref, g_ref, w_ref, a_ref, q_ref, out_ref, total):
    weight = jnp.concatenate([w_ref[o] for o in range(w_ref.shape[0])], axis=1)
    contract_last = (((1,), (1,)), ((), ()))
    total[...] = lax.dot_general(
        g_ref[...], weight, contract_last, preferred_element_type=jnp.float32
    )
    for j in range(out_ref.shape[0] // BLOCK):
        rows = pl.ds(j * BLOCK, BLOCK)
        extra = lax.dot_general(
            q_ref[rows, :], a_ref[index_ref[j]], contract_last, preferred_element_type=jnp.float32
        )
        out_ref[rows, :] = (total[rows, :] + extra).astype(out_ref.dtype)


def activation_grad(index, cotangent, weight, maps, q_low):
    rows, columns = cotangent.shape
    own_count, width, piece = weight.shape
    rank = maps.shape[2]
    tile = 256
    return pl.pallas_call(
        grad_body,
        grid_spec=pltpu.PrefetchScalarGridSpec(
            num_scalar_prefetch=1,
            grid=(width // tile,),
            in_specs=[
                pl.BlockSpec((rows, columns), lambda k, index_ref: (0, 0)),
                pl.BlockSpec((own_count, tile, piece), lambda k, index_ref: (0, k, 0)),
                pl.BlockSpec((own_count, tile, rank), lambda k, index_ref: (0, k, 0)),
                pl.BlockSpec((rows, rank), lambda k, index_ref: (0, 0)),
            ],
            out_specs=pl.BlockSpec((rows, tile), lambda k, index_ref: (0, k)),
            scratch_shapes=[pltpu.VMEM((rows, tile), jnp.float32)],
        ),
        out_shape=jax.ShapeDtypeStruct((rows, width), jnp.bfloat16),
        compiler_params=pltpu.CompilerParams(vmem_limit_bytes=40 * 1024 * 1024),
        cost_estimate=pl.CostEstimate(
            flops=2 * rows * width * (columns + rank),
            bytes_accessed=2 * (rows * columns + width * columns + rows * width),
            transcendentals=0,
        ),
    )(index, cotangent, weight, maps, q_low)


def after(value, *others):
    return lax.optimization_barrier((value,) + others)[0]


def shards(
    activations, cotangent, frozen_weight, down_weight, up_weight, slot_of_adapter, tenant_of_block
):
    own_count = lax.axis_size("own")
    own_index = lax.axis_index("own")
    fsdp_count = lax.axis_size("fsdp")
    fsdp_index = lax.axis_index("fsdp")
    tok_rows, width_part = activations.shape
    col_count = cotangent.shape[1]
    resident_count = down_weight.shape[0]
    paired_rank = down_weight.shape[2]
    rank_half = paired_rank // 2
    block_count = tok_rows // BLOCK
    slot_table = slot_of_adapter[tenant_of_block].reshape(own_count, block_count)
    owner_table = slot_table // resident_count
    local_table = slot_table % resident_count
    wanted_mask = owner_table == own_index
    wanted_any = jnp.any(wanted_mask, axis=1)
    wanted_local = jnp.max(jnp.where(wanted_mask, local_table, 0), axis=1)
    held_ids = jnp.arange(resident_count, dtype=jnp.int32)
    serve_mask = (wanted_local[:, None] == held_ids[None, :]) & wanted_any[:, None]
    my_owner = lax.dynamic_index_in_dim(owner_table, own_index, 0, keepdims=False)
    owner_ids = jnp.arange(own_count, dtype=jnp.int32)
    owner_rows = jnp.repeat(my_owner, BLOCK)
    row_mask = owner_ids[:, None] == owner_rows[None, :]

    def exchange(value):
        return lax.all_to_all(value, "own", split_axis=0, concat_axis=0, tiled=True)

    fetched_b = exchange(pick_rows(wanted_local, up_weight))
    outgoing_down = after(pick_rows(wanted_local, down_weight), fetched_b)
    fetched_a = exchange(outgoing_down)

    g_blocks = cotangent.reshape(block_count, BLOCK, col_count)
    block_b = fetched_b[my_owner]
    q_single = jnp.einsum(
        "btc,brc->btr", g_blocks, block_b, preferred_element_type=jnp.float32
    ).reshape(tok_rows, rank_half)
    q_all = lax.all_gather(q_single.astype(jnp.bfloat16), "fsdp", axis=0)
    q_low = (
        q_all.reshape(2, fsdp_count // 2, tok_rows, rank_half)
        .astype(jnp.float32)
        .sum(axis=1)
        .astype(jnp.bfloat16)
    )
    q_low = jnp.concatenate([q_low[0], q_low[1]], axis=1)
    q_wide = jnp.where(row_mask[:, :, None], q_low[None], jnp.bfloat16(0))

    part_a = jnp.einsum(
        "otr,td->ord", q_wide, activations, preferred_element_type=jnp.float32
    ).astype(jnp.bfloat16)
    late_weight, late_cotangent, part_a, outgoing_down = lax.optimization_barrier(
        (frozen_weight, cotangent, part_a, outgoing_down)
    )
    weight_rows, full_grad = gather(late_weight, late_cotangent)
    fetched_a, part_a, weight_rows = lax.optimization_barrier((fetched_a, part_a, weight_rows))
    back_a = exchange(part_a)

    inner_part = inner_product(my_owner, activations, fetched_a)
    inner_all = lax.all_gather(inner_part, "fsdp", axis=0)
    proj_index = fsdp_index * col_count // KEY_VALUE_WIDTH
    inner_mine = lax.dynamic_slice_in_dim(inner_all, proj_index * rank_half, rank_half, 2)
    inner_mine = inner_mine.astype(jnp.float32).sum(axis=0).astype(jnp.bfloat16)
    inner_wide = jnp.where(row_mask[:, :, None], inner_mine[None], jnp.bfloat16(0))
    part_b = jnp.einsum(
        "otr,tc->orc", inner_wide, cotangent, preferred_element_type=jnp.float32
    ).astype(jnp.bfloat16)

    activation_gradient = activation_grad(my_owner, full_grad, weight_rows, fetched_a, q_low)

    def accumulate(back):
        terms = jnp.where(serve_mask[:, :, None, None], back[:, None], jnp.bfloat16(0))
        return terms.astype(jnp.float32).sum(axis=0).astype(jnp.bfloat16)

    down_gradient = accumulate(after(back_a, activation_gradient)).transpose(0, 2, 1)
    back_b = exchange(after(part_b, back_a))
    up_gradient = accumulate(back_b)
    return (activation_gradient, down_gradient, up_gradient)


def solution(mesh):
    return jax.shard_map(
        shards,
        mesh=mesh,
        in_specs=(
            P("own", "fsdp"),
            P("own", "fsdp"),
            P("fsdp", "own"),
            P("own", "fsdp", None),
            P("own", None, "fsdp"),
            P(),
            P(),
        ),
        out_specs=(P("own", "fsdp"), P("own", "fsdp", None), P("own", None, "fsdp")),
        check_vma=False,
    )
```

```python
import functools

import jax
import jax.numpy as jnp
from jax import lax
from jax.experimental import pallas as pl
from jax.experimental.pallas import tpu as pltpu
from jax.sharding import PartitionSpec as P

KEY_VALUE_WIDTH = 1024
BLOCK = 128
MESH = pl.DeviceIdType.MESH


def inner_body(index_ref, x_ref, a_ref, out_ref):
    out_ref[...] = jnp.dot(x_ref[...], a_ref[0], preferred_element_type=jnp.float32).astype(
        out_ref.dtype
    )


def inner_product(index, tokens, maps):
    rows, width = tokens.shape
    rank = maps.shape[2]
    return pl.pallas_call(
        inner_body,
        grid_spec=pltpu.PrefetchScalarGridSpec(
            num_scalar_prefetch=1,
            grid=(index.shape[0],),
            in_specs=[
                pl.BlockSpec((BLOCK, width), lambda k, index_ref: (k, 0)),
                pl.BlockSpec((1, width, rank), lambda k, index_ref: (index_ref[k], 0, 0)),
            ],
            out_specs=pl.BlockSpec((BLOCK, rank), lambda k, index_ref: (k, 0)),
        ),
        out_shape=jax.ShapeDtypeStruct((rows, rank), jnp.bfloat16),
    )(index, tokens, maps)


def gather_body(
    chips, ring, wanted_ref, owner_ref, w_ref, g_ref, down_ref, up_ref,
    w_out, g_out, a_out, q_out,
    out_a, out_b, in_b, q_box,
    w_send, w_recv, f_send, f_recv, g_send, g_recv,
    a_send, a_recv, b_send, b_recv, q_send, q_recv, here,
):
    own = lax.axis_index("own")
    fsdp = lax.axis_index("fsdp")
    count = 2 * chips
    chip, core = own // 2, lax.rem(own, 2)
    sibling = chip * 2 + 1 - core
    columns = g_ref.shape[1]

    def chip_of(k):
        return lax.rem(chip + k, chips)

    def g_slice(f):
        return g_out.at[:, pl.ds(pl.multiple_of(f * columns, columns), columns)]

    keep_w = pltpu.make_async_copy(w_ref, w_out.at[own], here.at[0])
    keep_g = pltpu.make_async_copy(g_ref, g_slice(fsdp), here.at[1])
    keep_w.start()
    keep_g.start()

    def peer(k):
        return lax.rem(own + k, count)

    def source(k):
        return lax.rem(own + count - k, count)

    barrier = pltpu.get_barrier_semaphore()
    for k in range(1, count):
        pl.semaphore_signal(barrier, inc=1, device_id={"own": peer(k)}, device_id_type=MESH)
    for k in range(1, ring):
        pl.semaphore_signal(
            barrier, inc=1, device_id={"fsdp": lax.rem(fsdp + k, ring)}, device_id_type=MESH
        )
    for k in range(count):
        out_b[k] = up_ref[wanted_ref[peer(k)]]
    in_b[own] = out_b[0]
    pl.semaphore_wait(barrier, count + ring - 2)

    def b_copy(k, slot):
        return pltpu.make_async_remote_copy(
            src_ref=out_b.at[k],
            dst_ref=in_b.at[slot],
            send_sem=b_send.at[k - 1],
            recv_sem=b_recv.at[k - 1],
            device_id={"own": peer(k)},
            device_id_type=MESH,
        )

    def a_copy(k, slot):
        return pltpu.make_async_remote_copy(
            src_ref=out_a.at[k],
            dst_ref=a_out.at[slot],
            send_sem=a_send.at[k - 1],
            recv_sem=a_recv.at[k - 1],
            device_id={"own": peer(k)},
            device_id_type=MESH,
        )

    def q_copy(k, slot):
        return pltpu.make_async_remote_copy(
            src_ref=q_box.at[fsdp],
            dst_ref=q_box.at[slot],
            send_sem=q_send.at[k - 1],
            recv_sem=q_recv.at[k - 1],
            device_id={"fsdp": lax.rem(fsdp + k, ring)},
            device_id_type=MESH,
        )

    for k in range(1, count):
        b_copy(k, own).start()

    def g_copy(way, k):
        sign = 1 if way == 0 else -1
        origin = fsdp - sign * k
        return pltpu.make_async_remote_copy(
            src_ref=g_ref if k == 0 else g_slice(origin),
            dst_ref=g_slice(origin),
            send_sem=g_send.at[way, k],
            recv_sem=g_recv.at[way, k],
            device_id={"fsdp": fsdp + sign},
            device_id_type=MESH,
        )

    def g_arrival(way, k):
        sign = 1 if way == 0 else -1
        origin = fsdp - sign * (k + 1)
        return pltpu.make_async_remote_copy(
            src_ref=g_slice(origin),
            dst_ref=g_slice(origin),
            send_sem=g_send.at[way, k],
            recv_sem=g_recv.at[way, k],
            device_id={"fsdp": fsdp - sign},
            device_id_type=MESH,
        )

    def g_sends(way, k):
        if way == 0:
            return (fsdp >= k) & (fsdp < ring - 1)
        return (fsdp <= ring - 1 - k) & (fsdp > 0)

    def g_gets(way, k):
        return fsdp >= k + 1 if way == 0 else fsdp <= ring - 2 - k

    def w_copy(k):
        return pltpu.make_async_remote_copy(
            src_ref=w_ref,
            dst_ref=w_out.at[own],
            send_sem=w_send.at[k - 1],
            recv_sem=w_recv.at[k - 1],
            device_id={"own": chip_of(k) * 2 + core},
            device_id_type=MESH,
        )

    def w_origin(k, side):
        return lax.rem(chip + chips - k, chips) * 2 + side

    def w_forward(k):
        piece = w_origin(k, core)
        return pltpu.make_async_remote_copy(
            src_ref=w_ref if k == 0 else w_out.at[piece],
            dst_ref=w_out.at[piece],
            send_sem=f_send.at[k],
            recv_sem=f_recv.at[k],
            device_id={"own": sibling},
            device_id_type=MESH,
        )

    for way in range(2):
        @pl.when(g_sends(way, 0))
        def _():
            g_copy(way, 0).start()

    for k in range(1, chips):
        w_copy(k).start()
    w_forward(0).start()

    for k in list(range(1, count)) + [0]:
        out_a[k] = down_ref[wanted_ref[peer(k)]]
        if k:
            a_copy(k, own).start()
    keep_a = pltpu.make_async_copy(out_a.at[0], a_out.at[own], here.at[2])
    keep_a.start()

    for k in range(1, count):
        b_copy(k, source(k)).wait_recv()
    rows = g_ref.shape[0]
    half, rank = rows // 2, up_ref.shape[1]
    parts = []
    for j in range(rows // BLOCK):
        parts.append(
            lax.dot_general(
                g_ref[j * BLOCK : (j + 1) * BLOCK, :],
                in_b[owner_ref[j]],
                (((1,), (1,)), ((), ())),
                preferred_element_type=jnp.float32,
            )
        )
    mid = len(parts) // 2
    q_box[fsdp] = jnp.concatenate(
        [jnp.concatenate(parts[:mid], axis=0), jnp.concatenate(parts[mid:], axis=0)], axis=1
    ).astype(jnp.bfloat16)
    for k in range(1, ring):
        q_copy(k, fsdp).start()
    for k in range(1, ring):
        q_copy(k, lax.rem(fsdp + ring - k, ring)).wait_recv()
    sums = []
    for side in range(2):
        total = q_box[side * (ring // 2)].astype(jnp.float32)
        for f in range(1, ring // 2):
            total = total + q_box[side * (ring // 2) + f].astype(jnp.float32)
        sums.append(total)
    for part in range(2):
        lanes = slice(part * rank, (part + 1) * rank)
        q_out[part * half : (part + 1) * half, :] = jnp.concatenate(
            [sums[0][:, lanes], sums[1][:, lanes]], axis=1
        ).astype(q_out.dtype)

    for k in range(max(ring - 1, chips - 1)):
        if k < ring - 1:
            for way in range(2):
                @pl.when(g_gets(way, k))
                def _():
                    g_arrival(way, k).wait_recv()

                if k + 1 < ring - 1:
                    @pl.when(g_sends(way, k + 1))
                    def _():
                        g_copy(way, k + 1).start()
        if k < chips - 1:
            piece = w_origin(k + 1, core)
            pltpu.make_async_remote_copy(
                src_ref=w_ref,
                dst_ref=w_out.at[piece],
                send_sem=w_send.at[k],
                recv_sem=w_recv.at[k],
                device_id={"own": sibling},
                device_id_type=MESH,
            ).wait_recv()
            w_forward(k + 1).start()

    for k in range(chips):
        piece = w_origin(k, 1 - core)
        pltpu.make_async_remote_copy(
            src_ref=w_ref,
            dst_ref=w_out.at[piece],
            send_sem=f_send.at[k],
            recv_sem=f_recv.at[k],
            device_id={"own": sibling},
            device_id_type=MESH,
        ).wait_recv()
        w_forward(k).wait_send()
    for k in range(1, chips):
        w_copy(k).wait_send()
    for k in range(ring - 1):
        for way in range(2):
            @pl.when(g_sends(way, k))
            def _():
                g_copy(way, k).wait_send()
    for k in range(1, ring):
        q_copy(k, fsdp).wait_send()
    for k in range(1, count):
        a_copy(k, source(k)).wait_recv()
        a_copy(k, own).wait_send()
        b_copy(k, own).wait_send()
    keep_w.wait()
    keep_g.wait()
    keep_a.wait()


def gather(wanted, owner, weight, cotangent, down, up):
    own_count, ring = lax.axis_size("own"), lax.axis_size("fsdp")
    chips = own_count // 2
    rows, columns = cotangent.shape
    rank = down.shape[2]
    hbm = pl.BlockSpec(memory_space=pl.ANY)
    vmem = pl.BlockSpec(memory_space=pltpu.VMEM)
    smem = pl.BlockSpec(memory_space=pltpu.SMEM)
    dma = pltpu.SemaphoreType.DMA
    others = dma((own_count - 1,))
    return pl.pallas_call(
        functools.partial(gather_body, chips, ring),
        out_shape=(
            jax.ShapeDtypeStruct((own_count,) + weight.shape, weight.dtype),
            jax.ShapeDtypeStruct((rows, columns * ring), cotangent.dtype),
            jax.ShapeDtypeStruct((own_count,) + down.shape[1:], down.dtype),
            jax.ShapeDtypeStruct((rows, rank), jnp.bfloat16),
        ),
        in_specs=[smem, smem, hbm, vmem, vmem, vmem],
        out_specs=(hbm, hbm, hbm, vmem),
        scratch_shapes=[
            pltpu.VMEM((own_count,) + down.shape[1:], down.dtype),
            pltpu.VMEM((own_count,) + up.shape[1:], up.dtype),
            pltpu.VMEM((own_count,) + up.shape[1:], up.dtype),
            pltpu.VMEM((ring, rows // 2, rank), jnp.bfloat16),
            dma((chips - 1,)),
            dma((chips - 1,)),
            dma((chips,)),
            dma((chips,)),
            dma((2, ring - 1)),
            dma((2, ring - 1)),
            others,
            others,
            others,
            others,
            dma((ring - 1,)),
            dma((ring - 1,)),
            dma((3,)),
        ],
        compiler_params=pltpu.CompilerParams(
            collective_id=0, has_side_effects=True, vmem_limit_bytes=32 * 1024 * 1024
        ),
    )(wanted, owner, weight, cotangent, down, up)


def grad_body(index_ref, g_ref, w_ref, a_ref, q_ref, out_ref, total):
    weight = jnp.concatenate([w_ref[o] for o in range(w_ref.shape[0])], axis=1)
    contract_last = (((1,), (1,)), ((), ()))
    total[...] = lax.dot_general(
        g_ref[...], weight, contract_last, preferred_element_type=jnp.float32
    )
    for j in range(out_ref.shape[0] // BLOCK):
        rows = pl.ds(j * BLOCK, BLOCK)
        extra = lax.dot_general(
            q_ref[rows, :], a_ref[index_ref[j]], contract_last, preferred_element_type=jnp.float32
        )
        out_ref[rows, :] = (total[rows, :] + extra).astype(out_ref.dtype)


def activation_grad(index, cotangent, weight, maps, q_low):
    rows, columns = cotangent.shape
    own_count, width, piece = weight.shape
    rank = maps.shape[2]
    tile = 256
    return pl.pallas_call(
        grad_body,
        grid_spec=pltpu.PrefetchScalarGridSpec(
            num_scalar_prefetch=1,
            grid=(width // tile,),
            in_specs=[
                pl.BlockSpec((rows, columns), lambda k, index_ref: (0, 0)),
                pl.BlockSpec((own_count, tile, piece), lambda k, index_ref: (0, k, 0)),
                pl.BlockSpec((own_count, tile, rank), lambda k, index_ref: (0, k, 0)),
                pl.BlockSpec((rows, rank), lambda k, index_ref: (0, 0)),
            ],
            out_specs=pl.BlockSpec((rows, tile), lambda k, index_ref: (0, k)),
            scratch_shapes=[pltpu.VMEM((rows, tile), jnp.float32)],
        ),
        out_shape=jax.ShapeDtypeStruct((rows, width), jnp.bfloat16),
        compiler_params=pltpu.CompilerParams(vmem_limit_bytes=40 * 1024 * 1024),
        cost_estimate=pl.CostEstimate(
            flops=2 * rows * width * (columns + rank),
            bytes_accessed=2 * (rows * columns + width * columns + rows * width),
            transcendentals=0,
        ),
    )(index, cotangent, weight, maps, q_low)


def sum_body(mask_ref, back_ref, out_ref):
    count, held = back_ref.shape[0], out_ref.shape[0]
    for s in range(held):
        total = jnp.zeros(back_ref.shape[1:], jnp.float32)
        for b in range(count):
            term = back_ref[b].astype(jnp.float32)
            total = total + jnp.where(mask_ref[b * held + s] != 0, term, 0.0)
        out_ref[s] = total.T.astype(out_ref.dtype)


def sum_served(mask, back, held):
    count, rank, width = back.shape
    tile = 256
    return pl.pallas_call(
        sum_body,
        grid_spec=pltpu.PrefetchScalarGridSpec(
            num_scalar_prefetch=1,
            grid=(width // tile,),
            in_specs=[pl.BlockSpec((count, rank, tile), lambda k, mask_ref: (0, 0, k))],
            out_specs=pl.BlockSpec((held, tile, rank), lambda k, mask_ref: (0, k, 0)),
        ),
        out_shape=jax.ShapeDtypeStruct((held, width, rank), back.dtype),
    )(mask, back)


def after(value, *others):
    return lax.optimization_barrier((value,) + others)[0]


def shards(
    activations, cotangent, frozen_weight, down_weight, up_weight, slot_of_adapter, tenant_of_block
):
    own_count = lax.axis_size("own")
    own_index = lax.axis_index("own")
    fsdp_count = lax.axis_size("fsdp")
    fsdp_index = lax.axis_index("fsdp")
    tok_rows, width_part = activations.shape
    col_count = cotangent.shape[1]
    resident_count = down_weight.shape[0]
    paired_rank = down_weight.shape[2]
    rank_half = paired_rank // 2
    block_count = tok_rows // BLOCK
    slot_table = slot_of_adapter[tenant_of_block].reshape(own_count, block_count)
    owner_table = slot_table // resident_count
    local_table = slot_table % resident_count
    wanted_mask = owner_table == own_index
    wanted_any = jnp.any(wanted_mask, axis=1)
    wanted_local = jnp.max(jnp.where(wanted_mask, local_table, 0), axis=1)
    held_ids = jnp.arange(resident_count, dtype=jnp.int32)
    serve_mask = (wanted_local[:, None] == held_ids[None, :]) & wanted_any[:, None]
    my_owner = lax.dynamic_index_in_dim(owner_table, own_index, 0, keepdims=False)
    owner_ids = jnp.arange(own_count, dtype=jnp.int32)
    owner_rows = jnp.repeat(my_owner, BLOCK)
    row_mask = owner_ids[:, None] == owner_rows[None, :]

    def exchange(value):
        return lax.all_to_all(value, "own", split_axis=0, concat_axis=0, tiled=True)

    weight_rows, full_grad, fetched_a, q_low = gather(
        wanted_local, my_owner, frozen_weight, cotangent, down_weight, up_weight
    )
    q_wide = jnp.where(row_mask[:, :, None], q_low[None], jnp.bfloat16(0))

    part_a = jnp.einsum(
        "otr,td->ord", q_wide, activations, preferred_element_type=jnp.float32
    ).astype(jnp.bfloat16)
    back_a = exchange(part_a)

    inner_part = inner_product(my_owner, activations, fetched_a)
    inner_all = lax.all_gather(inner_part, "fsdp", axis=0)
    proj_index = fsdp_index * col_count // KEY_VALUE_WIDTH
    inner_mine = lax.dynamic_slice_in_dim(inner_all, proj_index * rank_half, rank_half, 2)
    inner_mine = inner_mine.astype(jnp.float32).sum(axis=0).astype(jnp.bfloat16)
    inner_wide = jnp.where(row_mask[:, :, None], inner_mine[None], jnp.bfloat16(0))
    part_b = jnp.einsum(
        "otr,tc->orc", inner_wide, cotangent, preferred_element_type=jnp.float32
    ).astype(jnp.bfloat16)

    activation_gradient = activation_grad(my_owner, full_grad, weight_rows, fetched_a, q_low)

    def accumulate(back):
        terms = jnp.where(serve_mask[:, :, None, None], back[:, None], jnp.bfloat16(0))
        return terms.astype(jnp.float32).sum(axis=0).astype(jnp.bfloat16)

    down_gradient = sum_served(
        serve_mask.astype(jnp.int32).reshape(-1),
        after(back_a, activation_gradient),
        resident_count,
    )
    back_b = exchange(after(part_b, back_a))
    up_gradient = accumulate(back_b)
    return (activation_gradient, down_gradient, up_gradient)


def solution(mesh):
    return jax.shard_map(
        shards,
        mesh=mesh,
        in_specs=(
            P("own", "fsdp"),
            P("own", "fsdp"),
            P("fsdp", "own"),
            P("own", "fsdp", None),
            P("own", None, "fsdp"),
            P(),
            P(),
        ),
        out_specs=(P("own", "fsdp"), P("own", "fsdp", None), P("own", None, "fsdp")),
        check_vma=False,
    )
```

```python
import functools

import jax
import jax.numpy as jnp
from jax import lax
from jax.experimental import pallas as pl
from jax.experimental.pallas import tpu as pltpu
from jax.sharding import PartitionSpec as P

KEY_VALUE_WIDTH = 1024
BLOCK = 128
MESH = pl.DeviceIdType.MESH


def inner_body(index_ref, x_ref, a_ref, out_ref):
    out_ref[...] = jnp.dot(x_ref[...], a_ref[0], preferred_element_type=jnp.float32).astype(
        out_ref.dtype
    )


def inner_product(index, tokens, maps):
    rows, width = tokens.shape
    rank = maps.shape[2]
    return pl.pallas_call(
        inner_body,
        grid_spec=pltpu.PrefetchScalarGridSpec(
            num_scalar_prefetch=1,
            grid=(index.shape[0],),
            in_specs=[
                pl.BlockSpec((BLOCK, width), lambda k, index_ref: (k, 0)),
                pl.BlockSpec((1, width, rank), lambda k, index_ref: (index_ref[k], 0, 0)),
            ],
            out_specs=pl.BlockSpec((BLOCK, rank), lambda k, index_ref: (k, 0)),
        ),
        out_shape=jax.ShapeDtypeStruct((rows, rank), jnp.bfloat16),
    )(index, tokens, maps)


def gather_body(
    chips, ring, wanted_ref, owner_ref, w_ref, g_ref, down_ref, up_ref, x_ref, line_ref,
    w_out, g_out, a_out, q_out, pa_out,
    out_a, out_b, in_b, q_box, x_held, pa_held,
    w_send, w_recv, f_send, f_recv, g_send, g_recv,
    a_send, a_recv, b_send, b_recv, q_send, q_recv, here,
):
    own = lax.axis_index("own")
    fsdp = lax.axis_index("fsdp")
    count = 2 * chips
    chip, core = own // 2, lax.rem(own, 2)
    sibling = chip * 2 + 1 - core
    columns = g_ref.shape[1]

    def chip_of(k):
        return lax.rem(chip + k, chips)

    def g_slice(f):
        return g_out.at[:, pl.ds(pl.multiple_of(f * columns, columns), columns)]

    keep_w = pltpu.make_async_copy(w_ref, w_out.at[own], here.at[0])
    keep_g = pltpu.make_async_copy(g_ref, g_slice(fsdp), here.at[1])
    keep_x = pltpu.make_async_copy(x_ref, x_held, here.at[3])
    keep_pa = pltpu.make_async_copy(pa_held, pa_out, here.at[4])
    keep_w.start()
    keep_g.start()
    keep_x.start()

    def peer(k):
        return lax.rem(own + k, count)

    def source(k):
        return lax.rem(own + count - k, count)

    barrier = pltpu.get_barrier_semaphore()
    for k in range(1, count):
        pl.semaphore_signal(barrier, inc=1, device_id={"own": peer(k)}, device_id_type=MESH)
    for k in range(1, ring):
        pl.semaphore_signal(
            barrier, inc=1, device_id={"fsdp": lax.rem(fsdp + k, ring)}, device_id_type=MESH
        )
    for k in range(count):
        out_b[k] = up_ref[wanted_ref[peer(k)]]
    in_b[own] = out_b[0]
    pl.semaphore_wait(barrier, count + ring - 2)

    def b_copy(k, slot):
        return pltpu.make_async_remote_copy(
            src_ref=out_b.at[k],
            dst_ref=in_b.at[slot],
            send_sem=b_send.at[k - 1],
            recv_sem=b_recv.at[k - 1],
            device_id={"own": peer(k)},
            device_id_type=MESH,
        )

    def a_copy(k, slot):
        return pltpu.make_async_remote_copy(
            src_ref=out_a.at[k],
            dst_ref=a_out.at[slot],
            send_sem=a_send.at[k - 1],
            recv_sem=a_recv.at[k - 1],
            device_id={"own": peer(k)},
            device_id_type=MESH,
        )

    def q_copy(k, slot):
        return pltpu.make_async_remote_copy(
            src_ref=q_box.at[fsdp],
            dst_ref=q_box.at[slot],
            send_sem=q_send.at[k - 1],
            recv_sem=q_recv.at[k - 1],
            device_id={"fsdp": lax.rem(fsdp + k, ring)},
            device_id_type=MESH,
        )

    for k in range(1, count):
        b_copy(k, own).start()

    def g_copy(way, k):
        sign = 1 if way == 0 else -1
        origin = fsdp - sign * k
        return pltpu.make_async_remote_copy(
            src_ref=g_ref if k == 0 else g_slice(origin),
            dst_ref=g_slice(origin),
            send_sem=g_send.at[way, k],
            recv_sem=g_recv.at[way, k],
            device_id={"fsdp": fsdp + sign},
            device_id_type=MESH,
        )

    def g_arrival(way, k):
        sign = 1 if way == 0 else -1
        origin = fsdp - sign * (k + 1)
        return pltpu.make_async_remote_copy(
            src_ref=g_slice(origin),
            dst_ref=g_slice(origin),
            send_sem=g_send.at[way, k],
            recv_sem=g_recv.at[way, k],
            device_id={"fsdp": fsdp - sign},
            device_id_type=MESH,
        )

    def g_sends(way, k):
        if way == 0:
            return (fsdp >= k) & (fsdp < ring - 1)
        return (fsdp <= ring - 1 - k) & (fsdp > 0)

    def g_gets(way, k):
        return fsdp >= k + 1 if way == 0 else fsdp <= ring - 2 - k

    def w_copy(k):
        return pltpu.make_async_remote_copy(
            src_ref=w_ref,
            dst_ref=w_out.at[own],
            send_sem=w_send.at[k - 1],
            recv_sem=w_recv.at[k - 1],
            device_id={"own": chip_of(k) * 2 + core},
            device_id_type=MESH,
        )

    def w_origin(k, side):
        return lax.rem(chip + chips - k, chips) * 2 + side

    def w_forward(k):
        piece = w_origin(k, core)
        return pltpu.make_async_remote_copy(
            src_ref=w_ref if k == 0 else w_out.at[piece],
            dst_ref=w_out.at[piece],
            send_sem=f_send.at[k],
            recv_sem=f_recv.at[k],
            device_id={"own": sibling},
            device_id_type=MESH,
        )

    for way in range(2):
        @pl.when(g_sends(way, 0))
        def _():
            g_copy(way, 0).start()

    for k in range(1, chips):
        w_copy(k).start()
    w_forward(0).start()

    for k in list(range(1, count)) + [0]:
        out_a[k] = down_ref[wanted_ref[peer(k)]]
        if k:
            a_copy(k, own).start()
    keep_a = pltpu.make_async_copy(out_a.at[0], a_out.at[own], here.at[2])
    keep_a.start()

    for k in range(1, count):
        b_copy(k, source(k)).wait_recv()
    rows = g_ref.shape[0]
    half, rank = rows // 2, up_ref.shape[1]
    parts = []
    for j in range(rows // BLOCK):
        parts.append(
            lax.dot_general(
                g_ref[j * BLOCK : (j + 1) * BLOCK, :],
                in_b[owner_ref[j]],
                (((1,), (1,)), ((), ())),
                preferred_element_type=jnp.float32,
            )
        )
    mid = len(parts) // 2
    q_box[fsdp] = jnp.concatenate(
        [jnp.concatenate(parts[:mid], axis=0), jnp.concatenate(parts[mid:], axis=0)], axis=1
    ).astype(jnp.bfloat16)
    for k in range(1, ring):
        q_copy(k, fsdp).start()
    for k in range(1, ring):
        q_copy(k, lax.rem(fsdp + ring - k, ring)).wait_recv()
    sums = []
    for side in range(2):
        total = q_box[side * (ring // 2)].astype(jnp.float32)
        for f in range(1, ring // 2):
            total = total + q_box[side * (ring // 2) + f].astype(jnp.float32)
        sums.append(total)
    for part in range(2):
        lanes = slice(part * rank, (part + 1) * rank)
        q_out[part * half : (part + 1) * half, :] = jnp.concatenate(
            [sums[0][:, lanes], sums[1][:, lanes]], axis=1
        ).astype(q_out.dtype)

    for k in range(max(ring - 1, chips - 1)):
        if k < ring - 1:
            for way in range(2):
                @pl.when(g_gets(way, k))
                def _():
                    g_arrival(way, k).wait_recv()

                if k + 1 < ring - 1:
                    @pl.when(g_sends(way, k + 1))
                    def _():
                        g_copy(way, k + 1).start()
        if k < chips - 1:
            piece = w_origin(k + 1, core)
            pltpu.make_async_remote_copy(
                src_ref=w_ref,
                dst_ref=w_out.at[piece],
                send_sem=w_send.at[k],
                recv_sem=w_recv.at[k],
                device_id={"own": sibling},
                device_id_type=MESH,
            ).wait_recv()
            w_forward(k + 1).start()

    keep_x.wait()
    turned = q_out[...].astype(jnp.float32).T

    def owner_step(o, carry):
        picked = jnp.where(line_ref[...] == o, turned, 0.0).astype(jnp.bfloat16)
        pa_held[o] = jnp.dot(
            picked, x_held[...], preferred_element_type=jnp.float32
        ).astype(pa_held.dtype)
        return carry

    lax.fori_loop(0, count, owner_step, 0)
    keep_pa.start()

    for k in range(chips):
        piece = w_origin(k, 1 - core)
        pltpu.make_async_remote_copy(
            src_ref=w_ref,
            dst_ref=w_out.at[piece],
            send_sem=f_send.at[k],
            recv_sem=f_recv.at[k],
            device_id={"own": sibling},
            device_id_type=MESH,
        ).wait_recv()
        w_forward(k).wait_send()
    for k in range(1, chips):
        w_copy(k).wait_send()
    for k in range(ring - 1):
        for way in range(2):
            @pl.when(g_sends(way, k))
            def _():
                g_copy(way, k).wait_send()
    for k in range(1, ring):
        q_copy(k, fsdp).wait_send()
    for k in range(1, count):
        a_copy(k, source(k)).wait_recv()
        a_copy(k, own).wait_send()
        b_copy(k, own).wait_send()
    keep_w.wait()
    keep_g.wait()
    keep_a.wait()
    keep_pa.wait()


def gather(wanted, owner, weight, cotangent, down, up, tokens, line):
    own_count, ring = lax.axis_size("own"), lax.axis_size("fsdp")
    chips = own_count // 2
    rows, columns = cotangent.shape
    rank = down.shape[2]
    hbm = pl.BlockSpec(memory_space=pl.ANY)
    vmem = pl.BlockSpec(memory_space=pltpu.VMEM)
    smem = pl.BlockSpec(memory_space=pltpu.SMEM)
    dma = pltpu.SemaphoreType.DMA
    others = dma((own_count - 1,))
    return pl.pallas_call(
        functools.partial(gather_body, chips, ring),
        out_shape=(
            jax.ShapeDtypeStruct((own_count,) + weight.shape, weight.dtype),
            jax.ShapeDtypeStruct((rows, columns * ring), cotangent.dtype),
            jax.ShapeDtypeStruct((own_count,) + down.shape[1:], down.dtype),
            jax.ShapeDtypeStruct((rows, rank), jnp.bfloat16),
            jax.ShapeDtypeStruct((own_count, rank, tokens.shape[1]), jnp.bfloat16),
        ),
        in_specs=[smem, smem, hbm, vmem, vmem, vmem, hbm, vmem],
        out_specs=(hbm, hbm, hbm, vmem, hbm),
        scratch_shapes=[
            pltpu.VMEM((own_count,) + down.shape[1:], down.dtype),
            pltpu.VMEM((own_count,) + up.shape[1:], up.dtype),
            pltpu.VMEM((own_count,) + up.shape[1:], up.dtype),
            pltpu.VMEM((ring, rows // 2, rank), jnp.bfloat16),
            pltpu.VMEM(tokens.shape, tokens.dtype),
            pltpu.VMEM((own_count, rank, tokens.shape[1]), jnp.bfloat16),
            dma((chips - 1,)),
            dma((chips - 1,)),
            dma((chips,)),
            dma((chips,)),
            dma((2, ring - 1)),
            dma((2, ring - 1)),
            others,
            others,
            others,
            others,
            dma((ring - 1,)),
            dma((ring - 1,)),
            dma((5,)),
        ],
        compiler_params=pltpu.CompilerParams(
            collective_id=0, has_side_effects=True, vmem_limit_bytes=60 * 1024 * 1024
        ),
    )(wanted, owner, weight, cotangent, down, up, tokens, line)


def grad_body(index_ref, g_ref, w_ref, a_ref, q_ref, out_ref, total):
    weight = jnp.concatenate([w_ref[o] for o in range(w_ref.shape[0])], axis=1)
    contract_last = (((1,), (1,)), ((), ()))
    total[...] = lax.dot_general(
        g_ref[...], weight, contract_last, preferred_element_type=jnp.float32
    )
    for j in range(out_ref.shape[0] // BLOCK):
        rows = pl.ds(j * BLOCK, BLOCK)
        extra = lax.dot_general(
            q_ref[rows, :], a_ref[index_ref[j]], contract_last, preferred_element_type=jnp.float32
        )
        out_ref[rows, :] = (total[rows, :] + extra).astype(out_ref.dtype)


def activation_grad(index, cotangent, weight, maps, q_low):
    rows, columns = cotangent.shape
    own_count, width, piece = weight.shape
    rank = maps.shape[2]
    tile = 256
    return pl.pallas_call(
        grad_body,
        grid_spec=pltpu.PrefetchScalarGridSpec(
            num_scalar_prefetch=1,
            grid=(width // tile,),
            in_specs=[
                pl.BlockSpec((rows, columns), lambda k, index_ref: (0, 0)),
                pl.BlockSpec((own_count, tile, piece), lambda k, index_ref: (0, k, 0)),
                pl.BlockSpec((own_count, tile, rank), lambda k, index_ref: (0, k, 0)),
                pl.BlockSpec((rows, rank), lambda k, index_ref: (0, 0)),
            ],
            out_specs=pl.BlockSpec((rows, tile), lambda k, index_ref: (0, k)),
            scratch_shapes=[pltpu.VMEM((rows, tile), jnp.float32)],
        ),
        out_shape=jax.ShapeDtypeStruct((rows, width), jnp.bfloat16),
        compiler_params=pltpu.CompilerParams(vmem_limit_bytes=40 * 1024 * 1024),
        cost_estimate=pl.CostEstimate(
            flops=2 * rows * width * (columns + rank),
            bytes_accessed=2 * (rows * columns + width * columns + rows * width),
            transcendentals=0,
        ),
    )(index, cotangent, weight, maps, q_low)


def sum_body(mask_ref, back_ref, out_ref):
    count, held = back_ref.shape[0], out_ref.shape[0]
    for s in range(held):
        total = jnp.zeros(back_ref.shape[1:], jnp.float32)
        for b in range(count):
            term = back_ref[b].astype(jnp.float32)
            total = total + jnp.where(mask_ref[b * held + s] != 0, term, 0.0)
        out_ref[s] = total.T.astype(out_ref.dtype)


def sum_served(mask, back, held):
    count, rank, width = back.shape
    tile = 256
    return pl.pallas_call(
        sum_body,
        grid_spec=pltpu.PrefetchScalarGridSpec(
            num_scalar_prefetch=1,
            grid=(width // tile,),
            in_specs=[pl.BlockSpec((count, rank, tile), lambda k, mask_ref: (0, 0, k))],
            out_specs=pl.BlockSpec((held, tile, rank), lambda k, mask_ref: (0, k, 0)),
        ),
        out_shape=jax.ShapeDtypeStruct((held, width, rank), back.dtype),
    )(mask, back)


def after(value, *others):
    return lax.optimization_barrier((value,) + others)[0]


def shards(
    activations, cotangent, frozen_weight, down_weight, up_weight, slot_of_adapter, tenant_of_block
):
    own_count = lax.axis_size("own")
    own_index = lax.axis_index("own")
    fsdp_count = lax.axis_size("fsdp")
    fsdp_index = lax.axis_index("fsdp")
    tok_rows, width_part = activations.shape
    col_count = cotangent.shape[1]
    resident_count = down_weight.shape[0]
    paired_rank = down_weight.shape[2]
    rank_half = paired_rank // 2
    block_count = tok_rows // BLOCK
    slot_table = slot_of_adapter[tenant_of_block].reshape(own_count, block_count)
    owner_table = slot_table // resident_count
    local_table = slot_table % resident_count
    wanted_mask = owner_table == own_index
    wanted_any = jnp.any(wanted_mask, axis=1)
    wanted_local = jnp.max(jnp.where(wanted_mask, local_table, 0), axis=1)
    held_ids = jnp.arange(resident_count, dtype=jnp.int32)
    serve_mask = (wanted_local[:, None] == held_ids[None, :]) & wanted_any[:, None]
    my_owner = lax.dynamic_index_in_dim(owner_table, own_index, 0, keepdims=False)
    owner_ids = jnp.arange(own_count, dtype=jnp.int32)
    owner_rows = jnp.repeat(my_owner, BLOCK)
    row_mask = owner_ids[:, None] == owner_rows[None, :]

    def exchange(value):
        return lax.all_to_all(value, "own", split_axis=0, concat_axis=0, tiled=True)

    weight_rows, full_grad, fetched_a, q_low, part_a = gather(
        wanted_local,
        my_owner,
        frozen_weight,
        cotangent,
        down_weight,
        up_weight,
        activations,
        owner_rows[None, :],
    )
    back_a = exchange(part_a)

    inner_part = inner_product(my_owner, activations, fetched_a)
    inner_all = lax.all_gather(inner_part, "fsdp", axis=0)
    activation_gradient = activation_grad(my_owner, full_grad, weight_rows, fetched_a, q_low)
    inner_all = after(inner_all, activation_gradient)
    proj_index = fsdp_index * col_count // KEY_VALUE_WIDTH
    inner_mine = lax.dynamic_slice_in_dim(inner_all, proj_index * rank_half, rank_half, 2)
    inner_mine = inner_mine.astype(jnp.float32).sum(axis=0).astype(jnp.bfloat16)
    inner_wide = jnp.where(row_mask[:, :, None], inner_mine[None], jnp.bfloat16(0))
    part_b = jnp.einsum(
        "otr,tc->orc", inner_wide, cotangent, preferred_element_type=jnp.float32
    ).astype(jnp.bfloat16)

    def accumulate(back):
        terms = jnp.where(serve_mask[:, :, None, None], back[:, None], jnp.bfloat16(0))
        return terms.astype(jnp.float32).sum(axis=0).astype(jnp.bfloat16)

    down_gradient = sum_served(
        serve_mask.astype(jnp.int32).reshape(-1),
        back_a,
        resident_count,
    )
    back_b = exchange(after(part_b, back_a))
    up_gradient = accumulate(back_b)
    return (activation_gradient, down_gradient, up_gradient)


def solution(mesh):
    return jax.shard_map(
        shards,
        mesh=mesh,
        in_specs=(
            P("own", "fsdp"),
            P("own", "fsdp"),
            P("fsdp", "own"),
            P("own", "fsdp", None),
            P("own", None, "fsdp"),
            P(),
            P(),
        ),
        out_specs=(P("own", "fsdp"), P("own", "fsdp", None), P("own", None, "fsdp")),
        check_vma=False,
    )
```
